256 devices in a mesh: chan: 32 (over z_lo, x, y), strip: 8 (over z_hi, core).
Axes of the slice: x: 4, y: 4, z: 8 (z_hi: 4, z_lo: 2; z = z_hi * 2 + z_lo), core: 2. Of those that a mesh axis runs over, the one named last changes fastest.
Arguments:
- voltages: bfloat16 [2048, 292864], P(('strip', 'chan')), may hold values from -6 to 6
- taps: float32 [16, 2048], replicated, may hold values from -1.5 to 1.5
Outputs:
- visibilities: bfloat16 [64, 4096, 4096], P('chan', 'strip')
The draws below stay inside these ranges and needn't reach their ends.
All inputs are finite; a program needn't handle non-finite values.
Results may differ from the reference program's by a relative error of at most 0.0076.
Values may be sent and summed in bfloat16 or wider, within the bound.
No kernel may reach another device: no remote copies, remote signals or barrier semaphores. Data moves between devices by JAX's collectives and lax.ppermute only.
A program may use at most 128 MiB of HBM per device.

```python
import math
import jax
import jax.numpy as jnp
from jax import lax

INPUTS = 2048
FRAME_LEN = 2048
TAPS = 16
CHANNELS = 64
SLAB0 = 384
FRAMES = 128
SAMPLES = 292864


def steps_of(own_key, extent, split, least, largest):
    def one(dim, parts):
        heights = jax.random.uniform(jax.random.fold_in(jax.random.fold_in(own_key, 6), dim), (parts,), jnp.float32, least / len(split), largest / len(split))
        return jnp.repeat(jnp.exp(heights), extent[dim] // parts).reshape((-1,) + (1,) * (len(extent) - dim - 1))

    factor_of = one(*split[0])
    for cut in split[1:]:
        factor_of = factor_of * one(*cut)
    return factor_of


def noise(own_key, extent, scale, limit, pieces=(), kind=jnp.bfloat16):
    drawn = scale * jax.random.normal(own_key, extent, jnp.float32)
    if pieces:
        drawn = drawn * steps_of(own_key, extent, pieces, -0.22, 0.18)
    return jnp.clip(drawn, -limit, limit).astype(kind)


def setup_inputs(seed: int = 0) -> dict:
    arg_keys = jax.random.split(jax.random.key(seed), 3)
    voltages = noise(arg_keys[0], (INPUTS, SAMPLES), 1.0, 6.0, ((0, 256),))
    taps = noise(arg_keys[1], (TAPS, FRAME_LEN), TAPS ** -0.5, 1.5, (), jnp.float32)
    return {"voltages": voltages, "taps": taps}


def slab_table(length, channels, first):
    sample = jnp.arange(length, dtype=jnp.int32)[:, None]
    channel_ids = (first + jnp.arange(channels, dtype=jnp.int32))[None, :]
    phase_index = (sample * channel_ids) % length
    angles = phase_index.astype(jnp.float32) * (2.0 * math.pi / length)
    norm_scale = (2.0 / length) ** 0.5
    return jnp.concatenate([jnp.cos(angles) * norm_scale, -jnp.sin(angles) * norm_scale], axis=1).astype(jnp.bfloat16)


def channelize(signal, taps, dft_table, frame_lo, frame_count):
    inputs_here = signal.shape[0]
    length = taps.shape[1]
    framed = signal.reshape(inputs_here, -1, length)
    filtered = jnp.zeros((inputs_here, frame_count, length), jnp.float32)
    for tap_index in range(taps.shape[0]):
        window = lax.slice_in_dim(framed, frame_lo + tap_index, frame_lo + tap_index + frame_count, axis=1)
        filtered = filtered + taps[tap_index] * window.astype(jnp.float32)
    flat = filtered.astype(jnp.bfloat16).reshape(inputs_here * frame_count, length)
    spectra = jnp.dot(flat, dft_table, preferred_element_type=jnp.float32).astype(jnp.bfloat16)
    channels = dft_table.shape[1] // 2
    spectra = spectra.reshape(inputs_here, frame_count, 2, channels)
    return jnp.transpose(spectra, (3, 0, 2, 1)).reshape(channels, 2 * inputs_here, frame_count)


def reference(voltages, taps):
    dft_table = slab_table(FRAME_LEN, CHANNELS, SLAB0)
    blocks = voltages.reshape(INPUTS // 8, 8, -1)
    spectra = lax.map(lambda input_block: channelize(input_block, taps, dft_table, 0, FRAMES), blocks)
    spectra = jnp.transpose(spectra, (1, 0, 2, 3)).reshape(CHANNELS, 2 * INPUTS, FRAMES)

    def correlate(slab_rows):
        product = jnp.dot(slab_rows, slab_rows.T, preferred_element_type=jnp.float32)
        return (product * (1.0 / FRAMES)).astype(jnp.bfloat16)

    return lax.map(correlate, spectra)
```

```python
import math

import jax
import jax.numpy as jnp
import ml_dtypes
import numpy as np
from jax import lax
from jax.experimental import pallas as pl
from jax.experimental.pallas import tpu as pltpu
from jax.sharding import Mesh
from jax.sharding import PartitionSpec as P

FRAME_LEN = 2048
CHANNELS = 64
SLAB0 = 384
FRAMES = 128
TAPS = 16
INPUTS_HERE = 8
LANES = 128
CHUNK = 128
PEERS = 32
OWN = CHANNELS // PEERS
ROWS = 2 * INPUTS_HERE
STRIP_ROWS = PEERS * ROWS
STRIPS = 8
VMEM_LIMIT = 48 * 2**20


def slab_table():
    sample = np.arange(FRAME_LEN, dtype=np.int64)[:, None]
    channel_ids = SLAB0 + np.arange(CHANNELS, dtype=np.int64)[None, :]
    phase_index = sample * channel_ids % FRAME_LEN
    angles = phase_index.astype(np.float32) * np.float32(2.0 * math.pi / FRAME_LEN)
    norm_scale = np.float32((2.0 / FRAME_LEN) ** 0.5)
    return np.concatenate(
        [np.cos(angles) * norm_scale, -np.sin(angles) * norm_scale], axis=1
    ).astype(ml_dtypes.bfloat16)


def channelize_kernel(
    volt_hbm, taps_hbm, table_hbm, out_ref, volt, taps, table, filtered, product, turned, sems
):
    parts = FRAMES // CHUNK
    lands = []
    low = 0
    for part in range(parts):
        high = (part + 1) * CHUNK + TAPS - 1
        span = pl.ds(low * FRAME_LEN, (high - low) * FRAME_LEN)
        lands.append(
            pltpu.make_async_copy(volt_hbm.at[:, span], volt.at[:, span], sems.at[part])
        )
        low = high
    taps_copy = pltpu.make_async_copy(taps_hbm, taps, sems.at[parts])
    table_copy = pltpu.make_async_copy(table_hbm, table, sems.at[parts + 1])
    taps_copy.start()
    for land in lands:
        land.start()
    table_copy.start()
    taps_copy.wait()
    for part in range(parts):
        first = part * CHUNK
        lands[part].wait()

        def column(tile, carry):
            lane = pl.multiple_of(tile * LANES, LANES)
            weights = [
                jnp.broadcast_to(taps[pl.ds(t, 1), pl.ds(lane, LANES)], (INPUTS_HERE, LANES))
                for t in range(TAPS)
            ]
            sums = {}
            before = None
            for g in range(CHUNK + TAPS - 1):
                start = pl.multiple_of((first + g) * FRAME_LEN + lane, LANES)
                sample = volt[:, pl.ds(start, LANES)].astype(jnp.float32)
                for t in range(TAPS):
                    f = g - t
                    if 0 <= f < CHUNK:
                        term = weights[t] * sample
                        sums[f] = sums[f] + term if f in sums else term
                f = g - (TAPS - 1)
                if f >= 0 and f % 2 == 0:
                    before = sums.pop(f)
                elif f >= 0:
                    pair = jnp.concatenate([before, sums.pop(f)], axis=0)
                    rows = pl.ds((first + f - 1) * INPUTS_HERE, 2 * INPUTS_HERE)
                    filtered[rows, pl.ds(lane, LANES)] = pair.astype(jnp.bfloat16)
            return carry

        lax.fori_loop(0, FRAME_LEN // LANES, column, 0)
    table_copy.wait()
    product[...] = jnp.dot(filtered[...], table[...], preferred_element_type=jnp.float32)
    for i in range(INPUTS_HERE):
        turned[i * LANES : (i + 1) * LANES, :] = product[
            pl.ds(i, FRAMES, stride=INPUTS_HERE), :
        ].T

    def channel(c, carry):
        out_ref[c] = turned[pl.ds(c, ROWS, stride=CHANNELS), :].astype(jnp.bfloat16)
        return carry

    lax.fori_loop(0, CHANNELS, channel, 0, unroll=16)


def channelize(volt, taps, table):
    parts = FRAMES // CHUNK
    return pl.pallas_call(
        channelize_kernel,
        out_shape=jax.ShapeDtypeStruct((CHANNELS, ROWS, FRAMES), jnp.bfloat16),
        in_specs=[pl.BlockSpec(memory_space=pl.ANY)] * 3,
        out_specs=pl.BlockSpec(memory_space=pltpu.VMEM),
        scratch_shapes=[
            pltpu.VMEM(volt.shape, jnp.bfloat16),
            pltpu.VMEM((TAPS, FRAME_LEN), jnp.float32),
            pltpu.VMEM((FRAME_LEN, 2 * CHANNELS), jnp.bfloat16),
            pltpu.VMEM((FRAMES * INPUTS_HERE, FRAME_LEN), jnp.bfloat16),
            pltpu.VMEM((FRAMES * INPUTS_HERE, 2 * CHANNELS), jnp.float32),
            pltpu.VMEM((FRAMES * INPUTS_HERE, FRAMES), jnp.float32),
            pltpu.SemaphoreType.DMA((parts + 2,)),
        ],
        compiler_params=pltpu.CompilerParams(vmem_limit_bytes=VMEM_LIMIT),
    )(volt, taps, table)


def correlate_kernel(*refs):
    blocks, out_hbm, stage, sems = refs[:STRIPS], refs[STRIPS], refs[STRIPS + 1], refs[STRIPS + 2]
    z_hi = lax.axis_index("z_hi")
    core = lax.axis_index("core")
    writes = [None, None]
    step = 0
    for ch in range(OWN):
        left = blocks[0][:, ch].reshape(STRIP_ROWS, FRAMES)
        for b in range(STRIPS):
            slot = step % 2
            strip = lax.rem(z_hi + STRIPS // 2 - b // 2, STRIPS // 2) * 2 + lax.rem(core + b % 2, 2)
            right = blocks[b][:, ch].reshape(STRIP_ROWS, FRAMES)
            got = lax.dot_general(
                left, right, (((1,), (1,)), ((), ())), preferred_element_type=jnp.float32
            )
            if writes[slot] is not None:
                writes[slot].wait()
            stage[slot] = (got * (1.0 / FRAMES)).astype(jnp.bfloat16)
            span = pl.ds(pl.multiple_of(strip * STRIP_ROWS, STRIP_ROWS), STRIP_ROWS)
            writes[slot] = pltpu.make_async_copy(
                stage.at[slot], out_hbm.at[ch, :, span], sems.at[slot]
            )
            writes[slot].start()
            step += 1
    for write in writes:
        write.wait()


def correlate(blocks):
    return pl.pallas_call(
        correlate_kernel,
        out_shape=jax.ShapeDtypeStruct((OWN, STRIP_ROWS, STRIPS * STRIP_ROWS), jnp.bfloat16),
        in_specs=[pl.BlockSpec(memory_space=pltpu.VMEM)] * STRIPS,
        out_specs=pl.BlockSpec(memory_space=pl.ANY),
        scratch_shapes=[
            pltpu.VMEM((2, STRIP_ROWS, STRIP_ROWS), jnp.bfloat16),
            pltpu.SemaphoreType.DMA((2,)),
        ],
        compiler_params=pltpu.CompilerParams(vmem_limit_bytes=VMEM_LIMIT),
    )(*blocks)


def shift(block, by):
    return lax.ppermute(block, "z_hi", [(i, (i + by) % 4) for i in range(4)])


def swap(block):
    return lax.ppermute(block, "core", [(0, 1), (1, 0)])


def shards(volt, taps):
    spectra = channelize(volt, taps, jnp.asarray(slab_table()))
    own = lax.all_to_all(spectra, ("z_lo", "x", "y"), split_axis=0, concat_axis=0, tiled=True)
    own = own.reshape(PEERS, OWN, ROWS, FRAMES)
    blocks = []
    for by in range(4):
        block = shift(own, by) if by else own
        blocks += [block, swap(block)]
    return correlate(blocks)


def solution(mesh):
    fine = Mesh(mesh.devices.reshape(2, 4, 4, 4, 2), ("z_lo", "x", "y", "z_hi", "core"))
    inputs = ("z_hi", "core", "z_lo", "x", "y")
    return jax.shard_map(
        shards,
        mesh=fine,
        in_specs=(P(inputs, None), P()),
        out_specs=P(("z_lo", "x", "y"), ("z_hi", "core"), None),
        check_vma=False,
    )
```

```python
import functools
import math

import jax
import jax.numpy as jnp
import ml_dtypes
import numpy as np
from jax import lax
from jax.experimental import pallas as pl
from jax.experimental.pallas import tpu as pltpu
from jax.sharding import Mesh
from jax.sharding import PartitionSpec as P

FRAME_LEN = 2048
CHANNELS = 64
SLAB0 = 384
FRAMES = 128
TAPS = 16
INPUTS_HERE = 8
LANES = 128
CHUNKS = (32, 96)
PEERS = 32
OWN = CHANNELS // PEERS
ROWS = 2 * INPUTS_HERE
STRIP_ROWS = PEERS * ROWS
STRIPS = 8
VMEM_LIMIT = 60 * 2**20
CORRELATE_LIMIT = 16 * 2**20


def slab_table():
    sample = np.arange(FRAME_LEN, dtype=np.int64)[:, None]
    channel_ids = SLAB0 + np.arange(CHANNELS, dtype=np.int64)[None, :]
    phase_index = sample * channel_ids % FRAME_LEN
    angles = phase_index.astype(np.float32) * np.float32(2.0 * math.pi / FRAME_LEN)
    norm_scale = np.float32((2.0 / FRAME_LEN) ** 0.5)
    return np.concatenate(
        [np.cos(angles) * norm_scale, -np.sin(angles) * norm_scale], axis=1
    ).astype(ml_dtypes.bfloat16)


def channelize_kernel(
    volt_hbm, taps_hbm, table_hbm, out_ref, volt, taps, table, filtered, product, turned, sems
):
    parts = len(CHUNKS)
    lands = []
    low = 0
    for part in range(parts):
        high = sum(CHUNKS[: part + 1]) + TAPS - 1
        span = pl.ds(low * FRAME_LEN, (high - low) * FRAME_LEN)
        lands.append(
            pltpu.make_async_copy(volt_hbm.at[:, span], volt.at[:, span], sems.at[part])
        )
        low = high
    taps_copy = pltpu.make_async_copy(taps_hbm, taps, sems.at[parts])
    table_copy = pltpu.make_async_copy(table_hbm, table, sems.at[parts + 1])
    taps_copy.start()
    for land in lands:
        land.start()
    table_copy.start()
    taps_copy.wait()
    for part in range(parts):
        first, size = sum(CHUNKS[:part]), CHUNKS[part]
        lands[part].wait()

        def column(tile, carry):
            lane = pl.multiple_of(tile * LANES, LANES)
            weights = [
                jnp.broadcast_to(taps[pl.ds(t, 1), pl.ds(lane, LANES)], (INPUTS_HERE, LANES))
                for t in range(TAPS)
            ]
            sums = {}
            before = None
            for g in range(size + TAPS - 1):
                start = pl.multiple_of((first + g) * FRAME_LEN + lane, LANES)
                sample = volt[:, pl.ds(start, LANES)].astype(jnp.float32)
                for t in range(TAPS):
                    f = g - t
                    if 0 <= f < size:
                        term = weights[t] * sample
                        sums[f] = sums[f] + term if f in sums else term
                f = g - (TAPS - 1)
                if f >= 0 and f % 2 == 0:
                    before = sums.pop(f)
                elif f >= 0:
                    pair = jnp.concatenate([before, sums.pop(f)], axis=0)
                    rows = pl.ds((first + f - 1) * INPUTS_HERE, 2 * INPUTS_HERE)
                    filtered[rows, pl.ds(lane, LANES)] = pair.astype(jnp.bfloat16)
            return carry

        lax.fori_loop(0, FRAME_LEN // LANES, column, 0)
    table_copy.wait()
    product[...] = jnp.dot(filtered[...], table[...], preferred_element_type=jnp.float32)
    for i in range(INPUTS_HERE):
        turned[i * LANES : (i + 1) * LANES, :] = product[
            pl.ds(i, FRAMES, stride=INPUTS_HERE), :
        ].T

    def channel(c, carry):
        out_ref[c] = turned[pl.ds(c, ROWS, stride=CHANNELS), :].astype(jnp.bfloat16)
        return carry

    lax.fori_loop(0, CHANNELS, channel, 0, unroll=16)


def channelize(volt, taps, table):
    parts = len(CHUNKS)
    return pl.pallas_call(
        channelize_kernel,
        out_shape=jax.ShapeDtypeStruct((CHANNELS, ROWS, FRAMES), jnp.bfloat16),
        in_specs=[pl.BlockSpec(memory_space=pl.ANY)] * 3,
        out_specs=pl.BlockSpec(memory_space=pltpu.VMEM),
        scratch_shapes=[
            pltpu.VMEM(volt.shape, jnp.bfloat16),
            pltpu.VMEM((TAPS, FRAME_LEN), jnp.float32),
            pltpu.VMEM((FRAME_LEN, 2 * CHANNELS), jnp.bfloat16),
            pltpu.VMEM((FRAMES * INPUTS_HERE, FRAME_LEN), jnp.bfloat16),
            pltpu.VMEM((FRAMES * INPUTS_HERE, 2 * CHANNELS), jnp.float32),
            pltpu.VMEM((FRAMES * INPUTS_HERE, FRAMES), jnp.float32),
            pltpu.SemaphoreType.DMA((parts + 2,)),
        ],
        compiler_params=pltpu.CompilerParams(vmem_limit_bytes=VMEM_LIMIT),
    )(volt, taps, table)


def correlate_kernel(places, held, *refs):
    count = len(places)
    left_ref, blocks = refs[0], refs[1 : count + 1]
    out_hbm, stage, sems = refs[count + 1 + held :]
    z_hi = lax.axis_index("z_hi")
    core = lax.axis_index("core")
    writes = []
    for (by, other), block in zip(places, blocks, strict=True):
        strip = lax.rem(z_hi + 4 + by * (2 * core - 1), 4) * 2 + lax.rem(core + other, 2)
        span = pl.ds(pl.multiple_of(strip * STRIP_ROWS, STRIP_ROWS), STRIP_ROWS)
        for ch in range(OWN):
            left = left_ref[:, ch].reshape(STRIP_ROWS, FRAMES)
            right = block[:, ch].reshape(STRIP_ROWS, FRAMES)
            got = lax.dot_general(
                left, right, (((1,), (1,)), ((), ())), preferred_element_type=jnp.float32
            )
            slot = len(writes)
            stage[slot] = (got * (1.0 / FRAMES)).astype(jnp.bfloat16)
            write = pltpu.make_async_copy(stage.at[slot], out_hbm.at[ch, :, span], sems.at[slot])
            write.start()
            writes.append(write)
    for write in writes:
        write.wait()


def correlate(left, blocks, places, held=None):
    count = len(blocks)
    operands = [left, *blocks] + ([] if held is None else [held])
    spaces = [pltpu.VMEM] * (count + 1) + ([] if held is None else [pl.ANY])
    return pl.pallas_call(
        functools.partial(correlate_kernel, places, 0 if held is None else 1),
        out_shape=jax.ShapeDtypeStruct((OWN, STRIP_ROWS, STRIPS * STRIP_ROWS), jnp.bfloat16),
        in_specs=[pl.BlockSpec(memory_space=space) for space in spaces],
        out_specs=pl.BlockSpec(memory_space=pl.ANY),
        scratch_shapes=[
            pltpu.VMEM((OWN * count, STRIP_ROWS, STRIP_ROWS), jnp.bfloat16),
            pltpu.SemaphoreType.DMA((OWN * count,)),
        ],
        input_output_aliases={} if held is None else {count + 1: 0},
        cost_estimate=pl.CostEstimate(flops=1, bytes_accessed=1, transcendentals=0),
        compiler_params=pltpu.CompilerParams(vmem_limit_bytes=CORRELATE_LIMIT),
    )(*operands)


def onward(block):
    way = [(2 * z + core, (z + (1, 3)[core]) % 4 * 2 + core) for z in range(4) for core in range(2)]
    return lax.ppermute(block, ("z_hi", "core"), way)


def swap(block):
    return lax.ppermute(block, "core", [(0, 1), (1, 0)])


def shards(volt, taps):
    spectra = channelize(volt, taps, jnp.asarray(slab_table()))
    own = lax.all_to_all(spectra, ("z_lo", "x", "y"), split_axis=0, concat_axis=0, tiled=True)
    own = own.reshape(PEERS, OWN, ROWS, FRAMES)
    sibling = swap(own)
    first = onward(own)
    out = correlate(own, [own, sibling], ((0, 0), (0, 1)))
    sibling, out = lax.optimization_barrier((sibling, out))
    second = onward(sibling)
    third = onward(first)
    first_other, second_other = swap(first), swap(second)
    out = correlate(own, [first], ((1, 0),), out)
    third, first_other, second, second_other, out = lax.optimization_barrier(
        (third, first_other, second, second_other, out)
    )
    third_other = swap(third)
    out = correlate(
        own,
        [first_other, second, second_other, third],
        ((-1, 1), (1, 1), (-1, 0), (2, 0)),
        out,
    )
    third_other, out = lax.optimization_barrier((third_other, out))
    return correlate(own, [third_other], ((2, 1),), out)


def solution(mesh):
    fine = Mesh(mesh.devices.reshape(2, 4, 4, 4, 2), ("z_lo", "x", "y", "z_hi", "core"))
    inputs = ("z_hi", "core", "z_lo", "x", "y")
    return jax.shard_map(
        shards,
        mesh=fine,
        in_specs=(P(inputs, None), P()),
        out_specs=P(("z_lo", "x", "y"), ("z_hi", "core"), None),
        check_vma=False,
    )
```

```python
import functools
import math

import jax
import jax.numpy as jnp
import ml_dtypes
import numpy as np
from jax import lax
from jax.experimental import pallas as pl
from jax.experimental.pallas import tpu as pltpu
from jax.sharding import Mesh
from jax.sharding import PartitionSpec as P

FRAME_LEN = 2048
CHANNELS = 64
SLAB0 = 384
FRAMES = 128
TAPS = 16
INPUTS_HERE = 8
LANES = 128
LEAST = 4
PEERS = 32
OWN = CHANNELS // PEERS
ROWS = 2 * INPUTS_HERE
STRIP_ROWS = PEERS * ROWS
STRIPS = 8
VMEM_LIMIT = 60 * 2**20
CORRELATE_LIMIT = 16 * 2**20


def slab_table():
    sample = np.arange(FRAME_LEN, dtype=np.int64)[:, None]
    channel_ids = SLAB0 + np.arange(CHANNELS, dtype=np.int64)[None, :]
    phase_index = sample * channel_ids % FRAME_LEN
    angles = phase_index.astype(np.float32) * np.float32(2.0 * math.pi / FRAME_LEN)
    norm_scale = np.float32((2.0 / FRAME_LEN) ** 0.5)
    return np.concatenate(
        [np.cos(angles) * norm_scale, -np.sin(angles) * norm_scale], axis=1
    ).astype(ml_dtypes.bfloat16)


def filter_of(taps, sample, least):
    known = {}
    if len(taps) <= least:

        def plain(n):
            if n not in known:
                total = None
                for s, tap in enumerate(taps):
                    value = sample(n - s)
                    if value is not None:
                        term = tap * value
                        total = term if total is None else total + term
                known[n] = total
            return known[n]

        return plain

    both = {}

    def even(m):
        return sample(2 * m)

    def odd(m):
        return sample(2 * m + 1)

    def joined(m):
        if m not in both:
            left, right = even(m), odd(m)
            both[m] = right if left is None else left + right
        return both[m]

    even_taps, odd_taps = taps[0::2], taps[1::2]
    joined_taps = [left + right for left, right in zip(even_taps, odd_taps, strict=True)]
    of_even = filter_of(even_taps, even, least)
    of_odd = filter_of(odd_taps, odd, least)
    of_joined = filter_of(joined_taps, joined, least)

    def split(n):
        if n not in known:
            m = n // 2
            if n % 2 == 0:
                known[n] = of_even(m) + of_odd(m - 1)
            else:
                known[n] = (of_joined(m) - of_even(m)) - of_odd(m)
        return known[n]

    return split


def channelize_kernel(
    volt_hbm, taps_hbm, table_hbm, out_ref, volt, taps, table, filtered, product, turned, sems
):
    tiles = FRAME_LEN // LANES

    def landing(tile):
        span = pl.ds(pl.multiple_of(tile * LANES, LANES), LANES)
        return pltpu.make_async_copy(
            volt_hbm.at[:, :, span], volt.at[:, :, span], sems.at[tile]
        )

    taps_copy = pltpu.make_async_copy(taps_hbm, taps, sems.at[tiles])
    table_copy = pltpu.make_async_copy(table_hbm, table, sems.at[tiles + 1])
    taps_copy.start()
    for tile in range(tiles):
        landing(tile).start()
    table_copy.start()
    taps_copy.wait()

    def column(tile, carry):
        landing(tile).wait()
        lane = pl.ds(pl.multiple_of(tile * LANES, LANES), LANES)
        weights = [
            jnp.broadcast_to(taps[pl.ds(TAPS - 1 - j, 1), lane], (INPUTS_HERE, LANES))
            for j in range(TAPS)
        ]
        loaded = {}

        def sample(n):
            if n < 1:
                return None
            if n not in loaded:
                loaded[n] = volt[n - 1, :, lane].astype(jnp.float32)
            return loaded[n]

        output = filter_of(weights, sample, LEAST)
        for f in range(0, FRAMES, 2):
            pair = jnp.concatenate([output(f + TAPS), output(f + TAPS + 1)], axis=0)
            filtered[f * INPUTS_HERE : (f + 2) * INPUTS_HERE, lane] = pair.astype(jnp.bfloat16)
        return carry

    lax.fori_loop(0, tiles, column, 0)
    table_copy.wait()
    product[...] = jnp.dot(filtered[...], table[...], preferred_element_type=jnp.float32)
    for i in range(INPUTS_HERE):
        turned[i * LANES : (i + 1) * LANES, :] = product[
            pl.ds(i, FRAMES, stride=INPUTS_HERE), :
        ].T

    def channel(c, carry):
        out_ref[c] = turned[pl.ds(c, ROWS, stride=CHANNELS), :].astype(jnp.bfloat16)
        return carry

    lax.fori_loop(0, CHANNELS, channel, 0, unroll=16)


def channelize(volt, taps, table):
    framed = jnp.transpose(volt.reshape(INPUTS_HERE, -1, FRAME_LEN), (1, 0, 2))
    return pl.pallas_call(
        channelize_kernel,
        out_shape=jax.ShapeDtypeStruct((CHANNELS, ROWS, FRAMES), jnp.bfloat16),
        in_specs=[pl.BlockSpec(memory_space=pl.ANY)] * 3,
        out_specs=pl.BlockSpec(memory_space=pltpu.VMEM),
        scratch_shapes=[
            pltpu.VMEM(framed.shape, jnp.bfloat16),
            pltpu.VMEM((TAPS, FRAME_LEN), jnp.float32),
            pltpu.VMEM((FRAME_LEN, 2 * CHANNELS), jnp.bfloat16),
            pltpu.VMEM((FRAMES * INPUTS_HERE, FRAME_LEN), jnp.bfloat16),
            pltpu.VMEM((FRAMES * INPUTS_HERE, 2 * CHANNELS), jnp.float32),
            pltpu.VMEM((FRAMES * INPUTS_HERE, FRAMES), jnp.float32),
            pltpu.SemaphoreType.DMA((FRAME_LEN // LANES + 2,)),
        ],
        compiler_params=pltpu.CompilerParams(vmem_limit_bytes=VMEM_LIMIT),
    )(framed, taps, table)


def correlate_kernel(places, held, *refs):
    count = len(places)
    left_ref, blocks = refs[0], refs[1 : count + 1]
    out_hbm, stage, sems = refs[count + 1 + held :]
    z_hi = lax.axis_index("z_hi")
    core = lax.axis_index("core")
    writes = []
    for (by, other), block in zip(places, blocks, strict=True):
        strip = lax.rem(z_hi + 4 + by * (2 * core - 1), 4) * 2 + lax.rem(core + other, 2)
        span = pl.ds(pl.multiple_of(strip * STRIP_ROWS, STRIP_ROWS), STRIP_ROWS)
        for ch in range(OWN):
            left = left_ref[:, ch].reshape(STRIP_ROWS, FRAMES)
            right = block[:, ch].reshape(STRIP_ROWS, FRAMES)
            got = lax.dot_general(
                left, right, (((1,), (1,)), ((), ())), preferred_element_type=jnp.float32
            )
            slot = len(writes)
            stage[slot] = (got * (1.0 / FRAMES)).astype(jnp.bfloat16)
            write = pltpu.make_async_copy(stage.at[slot], out_hbm.at[ch, :, span], sems.at[slot])
            write.start()
            writes.append(write)
    for write in writes:
        write.wait()


def correlate(left, blocks, places, held=None):
    count = len(blocks)
    operands = [left, *blocks] + ([] if held is None else [held])
    spaces = [pltpu.VMEM] * (count + 1) + ([] if held is None else [pl.ANY])
    return pl.pallas_call(
        functools.partial(correlate_kernel, places, 0 if held is None else 1),
        out_shape=jax.ShapeDtypeStruct((OWN, STRIP_ROWS, STRIPS * STRIP_ROWS), jnp.bfloat16),
        in_specs=[pl.BlockSpec(memory_space=space) for space in spaces],
        out_specs=pl.BlockSpec(memory_space=pl.ANY),
        scratch_shapes=[
            pltpu.VMEM((OWN * count, STRIP_ROWS, STRIP_ROWS), jnp.bfloat16),
            pltpu.SemaphoreType.DMA((OWN * count,)),
        ],
        input_output_aliases={} if held is None else {count + 1: 0},
        cost_estimate=pl.CostEstimate(flops=1, bytes_accessed=1, transcendentals=0),
        compiler_params=pltpu.CompilerParams(vmem_limit_bytes=CORRELATE_LIMIT),
    )(*operands)


def onward(block):
    way = [(2 * z + core, (z + (1, 3)[core]) % 4 * 2 + core) for z in range(4) for core in range(2)]
    return lax.ppermute(block, ("z_hi", "core"), way)


def swap(block):
    return lax.ppermute(block, "core", [(0, 1), (1, 0)])


def shards(volt, taps):
    spectra = channelize(volt, taps, jnp.asarray(slab_table()))
    own = lax.all_to_all(spectra, ("z_lo", "x", "y"), split_axis=0, concat_axis=0, tiled=True)
    own = own.reshape(PEERS, OWN, ROWS, FRAMES)
    sibling = swap(own)
    first = onward(own)
    out = correlate(own, [own, sibling], ((0, 0), (0, 1)))
    sibling, out = lax.optimization_barrier((sibling, out))
    second = onward(sibling)
    third = onward(first)
    first_other, second_other = swap(first), swap(second)
    out = correlate(own, [first], ((1, 0),), out)
    third, first_other, second, second_other, out = lax.optimization_barrier(
        (third, first_other, second, second_other, out)
    )
    third_other = swap(third)
    out = correlate(
        own,
        [first_other, second, second_other, third],
        ((-1, 1), (1, 1), (-1, 0), (2, 0)),
        out,
    )
    third_other, out = lax.optimization_barrier((third_other, out))
    return correlate(own, [third_other], ((2, 1),), out)


def solution(mesh):
    fine = Mesh(mesh.devices.reshape(2, 4, 4, 4, 2), ("z_lo", "x", "y", "z_hi", "core"))
    inputs = ("z_hi", "core", "z_lo", "x", "y")
    return jax.shard_map(
        shards,
        mesh=fine,
        in_specs=(P(inputs, None), P()),
        out_specs=P(("z_lo", "x", "y"), ("z_hi", "core"), None),
        check_vma=False,
    )
```

```python
import functools
import math

import jax
import jax.numpy as jnp
import ml_dtypes
import numpy as np
from jax import lax
from jax.experimental import pallas as pl
from jax.experimental.pallas import tpu as pltpu
from jax.sharding import Mesh
from jax.sharding import PartitionSpec as P

FRAME_LEN = 2048
CHANNELS = 64
SLAB0 = 384
FRAMES = 128
TAPS = 16
INPUTS_HERE = 8
LANES = 128
LEAST = 4
PEERS = 32
OWN = CHANNELS // PEERS
ROWS = 2 * INPUTS_HERE
STRIP_ROWS = PEERS * ROWS
STRIPS = 8
VMEM_LIMIT = 60 * 2**20
CORRELATE_LIMIT = 16 * 2**20


def slab_table():
    sample = np.arange(FRAME_LEN, dtype=np.int64)[:, None]
    channel_ids = SLAB0 + np.arange(CHANNELS, dtype=np.int64)[None, :]
    phase_index = sample * channel_ids % FRAME_LEN
    angles = phase_index.astype(np.float32) * np.float32(2.0 * math.pi / FRAME_LEN)
    norm_scale = np.float32((2.0 / FRAME_LEN) ** 0.5)
    return np.concatenate(
        [np.cos(angles) * norm_scale, -np.sin(angles) * norm_scale], axis=1
    ).astype(ml_dtypes.bfloat16)


def filter_of(taps, sample, least):
    known = {}
    if len(taps) <= least:

        def plain(n):
            if n not in known:
                total = None
                for s, tap in enumerate(taps):
                    value = sample(n - s)
                    if value is not None:
                        term = tap * value
                        total = term if total is None else total + term
                known[n] = total
            return known[n]

        return plain

    both = {}

    def even(m):
        return sample(2 * m)

    def odd(m):
        return sample(2 * m + 1)

    def joined(m):
        if m not in both:
            left, right = even(m), odd(m)
            both[m] = right if left is None else left + right
        return both[m]

    even_taps, odd_taps = taps[0::2], taps[1::2]
    joined_taps = [left + right for left, right in zip(even_taps, odd_taps, strict=True)]
    of_even = filter_of(even_taps, even, least)
    of_odd = filter_of(odd_taps, odd, least)
    of_joined = filter_of(joined_taps, joined, least)

    def split(n):
        if n not in known:
            m = n // 2
            if n % 2 == 0:
                known[n] = of_even(m) + of_odd(m - 1)
            else:
                known[n] = (of_joined(m) - of_even(m)) - of_odd(m)
        return known[n]

    return split


def channelize_kernel(
    volt_hbm, taps_hbm, table_hbm, out_ref, volt, taps, table, filtered, product, turned, sems
):
    tiles = FRAME_LEN // LANES

    def landing(tile):
        span = pl.ds(pl.multiple_of(tile * LANES, LANES), LANES)
        return pltpu.make_async_copy(
            volt_hbm.at[:, :, span], volt.at[:, :, span], sems.at[tile]
        )

    taps_copy = pltpu.make_async_copy(taps_hbm, taps, sems.at[tiles])
    table_copy = pltpu.make_async_copy(table_hbm, table, sems.at[tiles + 1])
    taps_copy.start()
    for tile in range(tiles):
        landing(tile).start()
    table_copy.start()
    taps_copy.wait()

    def column(tile, carry):
        landing(tile).wait()
        lane = pl.ds(pl.multiple_of(tile * LANES, LANES), LANES)
        weights = [
            jnp.broadcast_to(taps[pl.ds(TAPS - 1 - j, 1), lane], (INPUTS_HERE, LANES))
            for j in range(TAPS)
        ]
        loaded = {}

        def sample(n):
            if n < 1:
                return None
            if n not in loaded:
                loaded[n] = volt[n - 1, :, lane].astype(jnp.float32)
            return loaded[n]

        output = filter_of(weights, sample, LEAST)
        for f in range(0, FRAMES, 2):
            pair = jnp.concatenate([output(f + TAPS), output(f + TAPS + 1)], axis=0)
            filtered[f * INPUTS_HERE : (f + 2) * INPUTS_HERE, lane] = pair.astype(jnp.bfloat16)
        return carry

    lax.fori_loop(0, tiles, column, 0)
    table_copy.wait()
    product[...] = jnp.dot(filtered[...], table[...], preferred_element_type=jnp.float32)
    for i in range(INPUTS_HERE):
        turned[i * LANES : (i + 1) * LANES, :] = product[
            pl.ds(i, FRAMES, stride=INPUTS_HERE), :
        ].T

    def channel(c, carry):
        out_ref[c] = turned[pl.ds(c, ROWS, stride=CHANNELS), :].astype(jnp.bfloat16)
        return carry

    lax.fori_loop(0, CHANNELS, channel, 0, unroll=16)


def channelize(volt, taps, table):
    framed = jnp.transpose(volt.reshape(INPUTS_HERE, -1, FRAME_LEN), (1, 0, 2))
    return pl.pallas_call(
        channelize_kernel,
        out_shape=jax.ShapeDtypeStruct((CHANNELS, ROWS, FRAMES), jnp.bfloat16),
        in_specs=[pl.BlockSpec(memory_space=pl.ANY)] * 3,
        out_specs=pl.BlockSpec(memory_space=pltpu.VMEM),
        scratch_shapes=[
            pltpu.VMEM(framed.shape, jnp.bfloat16),
            pltpu.VMEM((TAPS, FRAME_LEN), jnp.float32),
            pltpu.VMEM((FRAME_LEN, 2 * CHANNELS), jnp.bfloat16),
            pltpu.VMEM((FRAMES * INPUTS_HERE, FRAME_LEN), jnp.bfloat16),
            pltpu.VMEM((FRAMES * INPUTS_HERE, 2 * CHANNELS), jnp.float32),
            pltpu.VMEM((FRAMES * INPUTS_HERE, FRAMES), jnp.float32),
            pltpu.SemaphoreType.DMA((FRAME_LEN // LANES + 2,)),
        ],
        compiler_params=pltpu.CompilerParams(vmem_limit_bytes=VMEM_LIMIT),
    )(framed, taps, table)


def correlate_kernel(places, held, *refs):
    count = len(places)
    left_ref, blocks = refs[0], refs[1 : count + 1]
    out_hbm, stage, sems = refs[count + 1 + held :]
    z_hi = lax.axis_index("z_hi")
    core = lax.axis_index("core")
    writes = []
    for (by, other), block in zip(places, blocks, strict=True):
        strip = lax.rem(z_hi + 4 + by * (2 * core - 1), 4) * 2 + lax.rem(core + other, 2)
        span = pl.ds(pl.multiple_of(strip * STRIP_ROWS, STRIP_ROWS), STRIP_ROWS)
        for ch in range(OWN):
            left = left_ref[:, ch].reshape(STRIP_ROWS, FRAMES)
            right = block[:, ch].reshape(STRIP_ROWS, FRAMES)
            got = lax.dot_general(
                left, right, (((1,), (1,)), ((), ())), preferred_element_type=jnp.float32
            )
            slot = len(writes)
            stage[slot] = (got * (1.0 / FRAMES)).astype(jnp.bfloat16)
            write = pltpu.make_async_copy(stage.at[slot], out_hbm.at[ch, :, span], sems.at[slot])
            write.start()
            writes.append(write)
    for write in writes:
        write.wait()


def correlate(left, blocks, places, held=None):
    count = len(blocks)
    operands = [left, *blocks] + ([] if held is None else [held])
    spaces = [pltpu.VMEM] * (count + 1) + ([] if held is None else [pl.ANY])
    return pl.pallas_call(
        functools.partial(correlate_kernel, places, 0 if held is None else 1),
        out_shape=jax.ShapeDtypeStruct((OWN, STRIP_ROWS, STRIPS * STRIP_ROWS), jnp.bfloat16),
        in_specs=[pl.BlockSpec(memory_space=space) for space in spaces],
        out_specs=pl.BlockSpec(memory_space=pl.ANY),
        scratch_shapes=[
            pltpu.VMEM((OWN * count, STRIP_ROWS, STRIP_ROWS), jnp.bfloat16),
            pltpu.SemaphoreType.DMA((OWN * count,)),
        ],
        input_output_aliases={} if held is None else {count + 1: 0},
        cost_estimate=pl.CostEstimate(flops=1, bytes_accessed=1, transcendentals=0),
        compiler_params=pltpu.CompilerParams(vmem_limit_bytes=CORRELATE_LIMIT),
    )(*operands)


def onward(block):
    way = [(2 * z + core, (z + (1, 3)[core]) % 4 * 2 + core) for z in range(4) for core in range(2)]
    return lax.ppermute(block, ("z_hi", "core"), way)


def swap(block):
    return lax.ppermute(block, "core", [(0, 1), (1, 0)])


def shards(volt, taps):
    spectra = channelize(volt, taps, jnp.asarray(slab_table()))
    own = lax.all_to_all(spectra, ("z_lo", "x", "y"), split_axis=0, concat_axis=0, tiled=True)
    own = own.reshape(PEERS, OWN, ROWS, FRAMES)
    sibling = swap(own)
    first = onward(own)
    out = correlate(own, [own, sibling], ((0, 0), (0, 1)))
    sibling, out = lax.optimization_barrier((sibling, out))
    second = onward(sibling)
    third = onward(first)
    first_other, second_other = swap(first), swap(second)
    out = correlate(
        own, [first, first_other, second], ((1, 0), (-1, 1), (1, 1)), out
    )
    third, second_other, out = lax.optimization_barrier((third, second_other, out))
    third_other = swap(third)
    out = correlate(own, [second_other, third], ((-1, 0), (2, 0)), out)
    third_other, out = lax.optimization_barrier((third_other, out))
    return correlate(own, [third_other], ((2, 1),), out)


def solution(mesh):
    fine = Mesh(mesh.devices.reshape(2, 4, 4, 4, 2), ("z_lo", "x", "y", "z_hi", "core"))
    inputs = ("z_hi", "core", "z_lo", "x", "y")
    return jax.shard_map(
        shards,
        mesh=fine,
        in_specs=(P(inputs, None), P()),
        out_specs=P(("z_lo", "x", "y"), ("z_hi", "core"), None),
        check_vma=False,
    )
```

```python
import functools
import math

import jax
import jax.numpy as jnp
import ml_dtypes
import numpy as np
from jax import lax
from jax.experimental import pallas as pl
from jax.experimental.pallas import tpu as pltpu
from jax.sharding import Mesh
from jax.sharding import PartitionSpec as P

FRAME_LEN = 2048
CHANNELS = 64
SLAB0 = 384
FRAMES = 128
TAPS = 16
INPUTS_HERE = 8
LANES = 128
LEAST = 4
PEERS = 32
OWN = CHANNELS // PEERS
ROWS = 2 * INPUTS_HERE
STRIP_ROWS = PEERS * ROWS
STRIPS = 8
VMEM_LIMIT = 60 * 2**20
CORRELATE_LIMIT = 16 * 2**20


def slab_table():
    sample = np.arange(FRAME_LEN, dtype=np.int64)[:, None]
    channel_ids = SLAB0 + np.arange(CHANNELS, dtype=np.int64)[None, :]
    phase_index = sample * channel_ids % FRAME_LEN
    angles = phase_index.astype(np.float32) * np.float32(2.0 * math.pi / FRAME_LEN)
    norm_scale = np.float32((2.0 / FRAME_LEN) ** 0.5)
    return np.concatenate(
        [np.cos(angles) * norm_scale, -np.sin(angles) * norm_scale], axis=1
    ).astype(ml_dtypes.bfloat16)


def filter_of(taps, sample, least):
    known = {}
    if len(taps) <= least:

        def plain(n):
            if n not in known:
                total = None
                for s, tap in enumerate(taps):
                    value = sample(n - s)
                    if value is not None:
                        term = tap * value
                        total = term if total is None else total + term
                known[n] = total
            return known[n]

        return plain

    both = {}

    def even(m):
        return sample(2 * m)

    def odd(m):
        return sample(2 * m + 1)

    def joined(m):
        if m not in both:
            left, right = even(m), odd(m)
            both[m] = right if left is None else left + right
        return both[m]

    even_taps, odd_taps = taps[0::2], taps[1::2]
    joined_taps = [left + right for left, right in zip(even_taps, odd_taps, strict=True)]
    of_even = filter_of(even_taps, even, least)
    of_odd = filter_of(odd_taps, odd, least)
    of_joined = filter_of(joined_taps, joined, least)

    def split(n):
        if n not in known:
            m = n // 2
            if n % 2 == 0:
                known[n] = of_even(m) + of_odd(m - 1)
            else:
                known[n] = (of_joined(m) - of_even(m)) - of_odd(m)
        return known[n]

    return split


def channelize_kernel(
    volt_hbm, taps_hbm, table_hbm, out_ref, volt, taps, table, filtered, product, turned, sems
):
    tiles = FRAME_LEN // LANES

    def landing(tile):
        span = pl.ds(pl.multiple_of(tile * LANES, LANES), LANES)
        return pltpu.make_async_copy(
            volt_hbm.at[:, :, span], volt.at[:, :, span], sems.at[tile]
        )

    taps_copy = pltpu.make_async_copy(taps_hbm, taps, sems.at[tiles])
    table_copy = pltpu.make_async_copy(table_hbm, table, sems.at[tiles + 1])
    taps_copy.start()
    for tile in range(tiles):
        landing(tile).start()
    table_copy.start()
    taps_copy.wait()

    def column(tile, carry):
        landing(tile).wait()
        lane = pl.ds(pl.multiple_of(tile * LANES, LANES), LANES)
        weights = [
            jnp.broadcast_to(taps[pl.ds(TAPS - 1 - j, 1), lane], (INPUTS_HERE, LANES))
            for j in range(TAPS)
        ]
        loaded = {}

        def sample(n):
            if n < 1:
                return None
            if n not in loaded:
                loaded[n] = volt[n - 1, :, lane].astype(jnp.float32)
            return loaded[n]

        output = filter_of(weights, sample, LEAST)
        for f in range(0, FRAMES, 2):
            pair = jnp.concatenate([output(f + TAPS), output(f + TAPS + 1)], axis=0)
            filtered[f * INPUTS_HERE : (f + 2) * INPUTS_HERE, lane] = pair.astype(jnp.bfloat16)
        return carry

    lax.fori_loop(0, tiles, column, 0)
    table_copy.wait()
    product[: FRAMES * INPUTS_HERE, :] = jnp.dot(filtered[...], table[...], preferred_element_type=jnp.float32)
    for i in range(INPUTS_HERE):
        turned[i * LANES : (i + 1) * LANES, :] = product[
            pl.ds(i, FRAMES, stride=INPUTS_HERE), :
        ].T

    def channel(c, carry):
        out_ref[c] = turned[pl.ds(c, ROWS, stride=CHANNELS), :].astype(jnp.bfloat16)
        return carry

    lax.fori_loop(0, CHANNELS, channel, 0, unroll=16)


def channelize(volt, taps, table):
    framed = jnp.transpose(volt.reshape(INPUTS_HERE, -1, FRAME_LEN), (1, 0, 2))
    return pl.pallas_call(
        channelize_kernel,
        out_shape=jax.ShapeDtypeStruct((CHANNELS, ROWS, FRAMES), jnp.bfloat16),
        in_specs=[pl.BlockSpec(memory_space=pl.ANY)] * 3,
        out_specs=pl.BlockSpec(memory_space=pltpu.VMEM),
        scratch_shapes=[
            pltpu.VMEM(framed.shape, jnp.bfloat16),
            pltpu.VMEM((TAPS, FRAME_LEN), jnp.float32),
            pltpu.VMEM((FRAME_LEN, 2 * CHANNELS), jnp.bfloat16),
            pltpu.VMEM((FRAMES * INPUTS_HERE, FRAME_LEN), jnp.bfloat16),
            pltpu.VMEM(((FRAMES + 1) * INPUTS_HERE, 2 * CHANNELS), jnp.float32),
            pltpu.VMEM(((ROWS + 1) * CHANNELS, FRAMES), jnp.float32),
            pltpu.SemaphoreType.DMA((FRAME_LEN // LANES + 2,)),
        ],
        compiler_params=pltpu.CompilerParams(vmem_limit_bytes=VMEM_LIMIT),
    )(framed, taps, table)


def correlate_kernel(places, held, *refs):
    count = len(places)
    left_ref, blocks = refs[0], refs[1 : count + 1]
    out_hbm, stage, sems = refs[count + 1 + held :]
    z_hi = lax.axis_index("z_hi")
    core = lax.axis_index("core")
    writes = []
    for (by, other), block in zip(places, blocks, strict=True):
        strip = lax.rem(z_hi + 4 + by * (2 * core - 1), 4) * 2 + lax.rem(core + other, 2)
        span = pl.ds(pl.multiple_of(strip * STRIP_ROWS, STRIP_ROWS), STRIP_ROWS)
        for ch in range(OWN):
            left = left_ref[:, ch].reshape(STRIP_ROWS, FRAMES)
            right = block[:, ch].reshape(STRIP_ROWS, FRAMES)
            got = lax.dot_general(
                left, right, (((1,), (1,)), ((), ())), preferred_element_type=jnp.float32
            )
            slot = len(writes)
            stage[slot] = (got * (1.0 / FRAMES)).astype(jnp.bfloat16)
            write = pltpu.make_async_copy(stage.at[slot], out_hbm.at[ch, :, span], sems.at[slot])
            write.start()
            writes.append(write)
    for write in writes:
        write.wait()


def correlate(left, blocks, places, held=None):
    count = len(blocks)
    operands = [left, *blocks] + ([] if held is None else [held])
    spaces = [pltpu.VMEM] * (count + 1) + ([] if held is None else [pl.ANY])
    return pl.pallas_call(
        functools.partial(correlate_kernel, places, 0 if held is None else 1),
        out_shape=jax.ShapeDtypeStruct((OWN, STRIP_ROWS, STRIPS * STRIP_ROWS), jnp.bfloat16),
        in_specs=[pl.BlockSpec(memory_space=space) for space in spaces],
        out_specs=pl.BlockSpec(memory_space=pl.ANY),
        scratch_shapes=[
            pltpu.VMEM((OWN * count, STRIP_ROWS, STRIP_ROWS), jnp.bfloat16),
            pltpu.SemaphoreType.DMA((OWN * count,)),
        ],
        input_output_aliases={} if held is None else {count + 1: 0},
        cost_estimate=pl.CostEstimate(flops=1, bytes_accessed=1, transcendentals=0),
        compiler_params=pltpu.CompilerParams(vmem_limit_bytes=CORRELATE_LIMIT),
    )(*operands)


def onward(block):
    way = [(2 * z + core, (z + (1, 3)[core]) % 4 * 2 + core) for z in range(4) for core in range(2)]
    return lax.ppermute(block, ("z_hi", "core"), way)


def swap(block):
    return lax.ppermute(block, "core", [(0, 1), (1, 0)])


def shards(volt, taps):
    spectra = channelize(volt, taps, jnp.asarray(slab_table()))
    own = lax.all_to_all(spectra, ("z_lo", "x", "y"), split_axis=0, concat_axis=0, tiled=True)
    own = own.reshape(PEERS, OWN, ROWS, FRAMES)
    sibling = swap(own)
    first = onward(own)
    out = correlate(own, [own, sibling], ((0, 0), (0, 1)))
    sibling, out = lax.optimization_barrier((sibling, out))
    second = onward(sibling)
    third = onward(first)
    first_other, second_other = swap(first), swap(second)
    out = correlate(
        own, [first, first_other, second], ((1, 0), (-1, 1), (1, 1)), out
    )
    third, second_other, out = lax.optimization_barrier((third, second_other, out))
    third_other = swap(third)
    out = correlate(own, [second_other, third], ((-1, 0), (2, 0)), out)
    third_other, out = lax.optimization_barrier((third_other, out))
    return correlate(own, [third_other], ((2, 1),), out)


def solution(mesh):
    fine = Mesh(mesh.devices.reshape(2, 4, 4, 4, 2), ("z_lo", "x", "y", "z_hi", "core"))
    inputs = ("z_hi", "core", "z_lo", "x", "y")
    return jax.shard_map(
        shards,
        mesh=fine,
        in_specs=(P(inputs, None), P()),
        out_specs=P(("z_lo", "x", "y"), ("z_hi", "core"), None),
        check_vma=False,
    )
```

```python
import functools
import math

import jax
import jax.numpy as jnp
import ml_dtypes
import numpy as np
from jax import lax
from jax.experimental import pallas as pl
from jax.experimental.pallas import tpu as pltpu
from jax.sharding import Mesh
from jax.sharding import PartitionSpec as P

FRAME_LEN = 2048
CHANNELS = 64
SLAB0 = 384
FRAMES = 128
TAPS = 16
INPUTS_HERE = 8
LANES = 128
LEAST = 4
PEERS = 32
OWN = CHANNELS // PEERS
ROWS = 2 * INPUTS_HERE
STRIP_ROWS = PEERS * ROWS
STRIPS = 8
PARTS = 2
VMEM_LIMIT = 60 * 2**20
CORRELATE_LIMIT = 16 * 2**20


def slab_table():
    sample = np.arange(FRAME_LEN, dtype=np.int64)[:, None]
    channel_ids = SLAB0 + np.arange(CHANNELS, dtype=np.int64)[None, :]
    phase_index = sample * channel_ids % FRAME_LEN
    angles = phase_index.astype(np.float32) * np.float32(2.0 * math.pi / FRAME_LEN)
    norm_scale = np.float32((2.0 / FRAME_LEN) ** 0.5)
    return np.concatenate(
        [np.cos(angles) * norm_scale, -np.sin(angles) * norm_scale], axis=1
    ).astype(ml_dtypes.bfloat16)


def filter_of(taps, sample, least):
    known = {}
    if len(taps) <= least:

        def plain(n):
            if n not in known:
                total = None
                for s, tap in enumerate(taps):
                    value = sample(n - s)
                    if value is not None:
                        term = tap * value
                        total = term if total is None else total + term
                known[n] = total
            return known[n]

        return plain

    both = {}

    def even(m):
        return sample(2 * m)

    def odd(m):
        return sample(2 * m + 1)

    def joined(m):
        if m not in both:
            left, right = even(m), odd(m)
            both[m] = right if left is None else left + right
        return both[m]

    even_taps, odd_taps = taps[0::2], taps[1::2]
    joined_taps = [left + right for left, right in zip(even_taps, odd_taps, strict=True)]
    of_even = filter_of(even_taps, even, least)
    of_odd = filter_of(odd_taps, odd, least)
    of_joined = filter_of(joined_taps, joined, least)

    def split(n):
        if n not in known:
            m = n // 2
            if n % 2 == 0:
                known[n] = of_even(m) + of_odd(m - 1)
            else:
                known[n] = (of_joined(m) - of_even(m)) - of_odd(m)
        return known[n]

    return split


def channelize_kernel(
    volt_hbm, taps_hbm, table_hbm, out_ref, volt, taps, table, filtered, product, turned, sems
):
    tiles = FRAME_LEN // LANES

    def landing(tile):
        span = pl.ds(pl.multiple_of(tile * LANES, LANES), LANES)
        return pltpu.make_async_copy(
            volt_hbm.at[:, :, span], volt.at[:, :, span], sems.at[tile]
        )

    taps_copy = pltpu.make_async_copy(taps_hbm, taps, sems.at[tiles])
    table_copy = pltpu.make_async_copy(table_hbm, table, sems.at[tiles + 1])
    taps_copy.start()
    for tile in range(tiles):
        landing(tile).start()
    table_copy.start()
    taps_copy.wait()

    def column(tile, carry):
        landing(tile).wait()
        lane = pl.ds(pl.multiple_of(tile * LANES, LANES), LANES)
        weights = [
            jnp.broadcast_to(taps[pl.ds(TAPS - 1 - j, 1), lane], (INPUTS_HERE, LANES))
            for j in range(TAPS)
        ]
        loaded = {}

        def sample(n):
            if n < 1:
                return None
            if n not in loaded:
                loaded[n] = volt[n - 1, :, lane].astype(jnp.float32)
            return loaded[n]

        output = filter_of(weights, sample, LEAST)
        for f in range(0, FRAMES, 2):
            pair = jnp.concatenate([output(f + TAPS), output(f + TAPS + 1)], axis=0)
            filtered[f * INPUTS_HERE : (f + 2) * INPUTS_HERE, lane] = pair.astype(jnp.bfloat16)
        return carry

    lax.fori_loop(0, tiles, column, 0)
    table_copy.wait()
    product[: FRAMES * INPUTS_HERE, :] = jnp.dot(filtered[...], table[...], preferred_element_type=jnp.float32)
    for i in range(INPUTS_HERE):
        turned[i * LANES : (i + 1) * LANES, :] = product[
            pl.ds(i, FRAMES, stride=INPUTS_HERE), :
        ].T

    def channel(c, carry):
        out_ref[c] = turned[pl.ds(c, ROWS, stride=CHANNELS), :].astype(jnp.bfloat16)
        return carry

    lax.fori_loop(0, CHANNELS, channel, 0, unroll=16)


def channelize(volt, taps, table):
    framed = jnp.transpose(volt.reshape(INPUTS_HERE, -1, FRAME_LEN), (1, 0, 2))
    return pl.pallas_call(
        channelize_kernel,
        out_shape=jax.ShapeDtypeStruct((CHANNELS, ROWS, FRAMES), jnp.bfloat16),
        in_specs=[pl.BlockSpec(memory_space=pl.ANY)] * 3,
        out_specs=pl.BlockSpec(memory_space=pltpu.VMEM),
        scratch_shapes=[
            pltpu.VMEM(framed.shape, jnp.bfloat16),
            pltpu.VMEM((TAPS, FRAME_LEN), jnp.float32),
            pltpu.VMEM((FRAME_LEN, 2 * CHANNELS), jnp.bfloat16),
            pltpu.VMEM((FRAMES * INPUTS_HERE, FRAME_LEN), jnp.bfloat16),
            pltpu.VMEM(((FRAMES + 1) * INPUTS_HERE, 2 * CHANNELS), jnp.float32),
            pltpu.VMEM(((ROWS + 1) * CHANNELS, FRAMES), jnp.float32),
            pltpu.SemaphoreType.DMA((FRAME_LEN // LANES + 2,)),
        ],
        compiler_params=pltpu.CompilerParams(vmem_limit_bytes=VMEM_LIMIT),
    )(framed, taps, table)


def correlate_kernel(places, held, *refs):
    count = len(places)
    left_ref, blocks = refs[0], refs[1 : count + 1]
    out_hbm, stage, sems = refs[count + 1 + held :]
    z_hi = lax.axis_index("z_hi")
    core = lax.axis_index("core")
    writes = []
    for (by, other), block in zip(places, blocks, strict=True):
        strip = lax.rem(z_hi + 4 + by * (2 * core - 1), 4) * 2 + lax.rem(core + other, 2)
        span = pl.ds(pl.multiple_of(strip * STRIP_ROWS, STRIP_ROWS), STRIP_ROWS)
        for ch in range(OWN):
            left = left_ref[:, ch].reshape(STRIP_ROWS, FRAMES)
            right = block[:, ch].reshape(STRIP_ROWS, FRAMES)
            for part in range(PARTS):
                slot = len(writes)
                rows = slice(part * STRIP_ROWS // PARTS, (part + 1) * STRIP_ROWS // PARTS)
                got = lax.dot_general(
                    left[rows],
                    right,
                    (((1,), (1,)), ((), ())),
                    preferred_element_type=jnp.float32,
                )
                stage[slot] = (got * (1.0 / FRAMES)).astype(jnp.bfloat16)
                write = pltpu.make_async_copy(
                    stage.at[slot], out_hbm.at[ch, rows, span], sems.at[slot]
                )
                write.start()
                writes.append(write)
    for write in writes:
        write.wait()


def correlate(left, blocks, places, held=None):
    count = len(blocks)
    operands = [left, *blocks] + ([] if held is None else [held])
    spaces = [pltpu.VMEM] * (count + 1) + ([] if held is None else [pl.ANY])
    return pl.pallas_call(
        functools.partial(correlate_kernel, places, 0 if held is None else 1),
        out_shape=jax.ShapeDtypeStruct((OWN, STRIP_ROWS, STRIPS * STRIP_ROWS), jnp.bfloat16),
        in_specs=[pl.BlockSpec(memory_space=space) for space in spaces],
        out_specs=pl.BlockSpec(memory_space=pl.ANY),
        scratch_shapes=[
            pltpu.VMEM((OWN * count * PARTS, STRIP_ROWS // PARTS, STRIP_ROWS), jnp.bfloat16),
            pltpu.SemaphoreType.DMA((OWN * count * PARTS,)),
        ],
        input_output_aliases={} if held is None else {count + 1: 0},
        cost_estimate=pl.CostEstimate(flops=1, bytes_accessed=1, transcendentals=0),
        compiler_params=pltpu.CompilerParams(vmem_limit_bytes=CORRELATE_LIMIT),
    )(*operands)


def onward(block):
    way = [(2 * z + core, (z + (1, 3)[core]) % 4 * 2 + core) for z in range(4) for core in range(2)]
    return lax.ppermute(block, ("z_hi", "core"), way)


def swap(block):
    return lax.ppermute(block, "core", [(0, 1), (1, 0)])


def shards(volt, taps):
    spectra = channelize(volt, taps, jnp.asarray(slab_table()))
    own = lax.all_to_all(spectra, ("z_lo", "x", "y"), split_axis=0, concat_axis=0, tiled=True)
    own = own.reshape(PEERS, OWN, ROWS, FRAMES)
    sibling = swap(own)
    first = onward(own)
    out = correlate(own, [own, sibling], ((0, 0), (0, 1)))
    sibling, out = lax.optimization_barrier((sibling, out))
    second = onward(sibling)
    third = onward(first)
    first_other, second_other = swap(first), swap(second)
    out = correlate(
        own, [first, first_other, second], ((1, 0), (-1, 1), (1, 1)), out
    )
    third, second_other, out = lax.optimization_barrier((third, second_other, out))
    third_other = swap(third)
    out = correlate(own, [second_other, third], ((-1, 0), (2, 0)), out)
    third_other, out = lax.optimization_barrier((third_other, out))
    return correlate(own, [third_other], ((2, 1),), out)


def solution(mesh):
    fine = Mesh(mesh.devices.reshape(2, 4, 4, 4, 2), ("z_lo", "x", "y", "z_hi", "core"))
    inputs = ("z_hi", "core", "z_lo", "x", "y")
    return jax.shard_map(
        shards,
        mesh=fine,
        in_specs=(P(inputs, None), P()),
        out_specs=P(("z_lo", "x", "y"), ("z_hi", "core"), None),
        check_vma=False,
    )
```
